32 devices in a mesh: inst: 8 (over z, y), tp: 4 (over x, core).
Axes of the slice: x: 2, y: 2, z: 4, core: 2. Of those that a mesh axis runs over, the one named last changes fastest.
Arguments:
- ssm_state: bfloat16 [112, 128, 64, 128], P('inst', 'tp'), may hold values from -6 to 6
- conv_x: bfloat16 [112, 3, 8192], P('inst', None, 'tp'), may hold values from -6 to 6
- conv_bc: bfloat16 [112, 3, 1024], P('inst', None, 'tp'), may hold values from -6 to 6
- k_cache: bfloat16 [112, 64, 1024], P('inst', None, 'tp'), may hold values from -5 to 5
- v_cache: bfloat16 [112, 64, 1024], P('inst', None, 'tp'), may hold values from -5 to 5
- context_len: int32 [112], P('inst'), may hold values from 1 to 61, as said below
- dest_inst: int32 [112], P('inst'), may hold values from 0 to 7, as said below
- dest_slot: int32 [112], P('inst'), may hold values from 0 to 13, as said below
- x_in: bfloat16 [3, 112, 8192], P(None, 'inst', 'tp'), may hold values from -6 to 6
- bc_in: bfloat16 [3, 112, 1024], P(None, 'inst', 'tp'), may hold values from -6 to 6
- z_in: bfloat16 [3, 112, 8192], P(None, 'inst', 'tp'), may hold values from -6 to 6
- dt_in: float32 [3, 112, 128], P(None, 'inst', 'tp'), may hold values from -4 to 4
- q_in: bfloat16 [3, 112, 4096], P(None, 'inst', 'tp'), may hold values from -100 to 100
- k_in: bfloat16 [3, 112, 1024], P(None, 'inst', 'tp'), may hold values from -5 to 5
- v_in: bfloat16 [3, 112, 1024], P(None, 'inst', 'tp'), may hold values from -5 to 5
- conv_wx: float32 [4, 8192], P(None, 'tp'), may hold values from -3 to 3
- conv_wbc: float32 [4, 1024], P(None, 'tp'), may hold values from -3 to 3
- a_rate: float32 [128], P('tp'), may hold values from 0.02 to 3
- dt_bias: float32 [128], P('tp'), may hold values from -1 to 1
- d_skip: float32 [128], P('tp'), may hold values from 1 to 4
- norm_gain: bfloat16 [8192], P('tp'), may hold values from 0.5 to 1.5
- o_proj: bfloat16 [4096, 4096], P('tp'), may hold values from -0.09375 to 0.09375
Outputs:
- ssm_final: bfloat16 [112, 128, 64, 128], P('inst', 'tp')
- convx_final: bfloat16 [112, 3, 8192], P('inst', None, 'tp')
- convbc_final: bfloat16 [112, 3, 1024], P('inst', None, 'tp')
- k_final: bfloat16 [112, 64, 1024], P('inst', None, 'tp')
- v_final: bfloat16 [112, 64, 1024], P('inst', None, 'tp')
- mamba_out: bfloat16 [3, 112, 8192], P(None, 'inst', 'tp')
- attn_out: bfloat16 [3, 112, 4096], P(None, 'inst', 'tp')
The draws below stay inside these ranges and needn't reach their ends.
Inputs may be any that keep to these rules, and one draw needn't show every extreme that they name: Row r's request moves to row dest_inst * 14 + dest_slot; this map is a permutation of all rows. A request that stays keeps its slot. At every instance exactly one request stays, 13 leave and 13 arrive; an instance sends at most 2 requests to any other instance, and every instance sends exactly 2 to some other. `dest_slot`: see dest_inst. `context_len`: some row has exactly 61, some exactly 1.
All inputs are finite; a program needn't handle non-finite values.
Results may differ from the reference program's by a relative error of at most 0.011.
Values may be sent and summed in bfloat16 or wider, within the bound.
A program may use at most 192 MiB of HBM per device.

```python
import math
import jax
import jax.numpy as jnp
from jax import lax

SLOTS = 14
CACHE = 64
STEPS = 3
MHEADS = 128
HEAD_P = 64
STATE_N = 128
GROUPS = 4
CONV = 4
QHEADS = 32
KVHEADS = 8
HEAD_DIM = 128
D = 4096
ROWS = 112


def plan_tables(key):
    count = ROWS // SLOTS
    order = jax.random.permutation(jax.random.fold_in(key, 101), count).astype(jnp.int32)
    place = jnp.argsort(order).astype(jnp.int32)
    row_keys = jax.random.split(jax.random.fold_in(key, 104), count)
    slot_perm = jax.vmap(lambda one_key: jax.random.permutation(one_key, SLOTS))(row_keys).astype(jnp.int32)
    offset = jnp.argsort(slot_perm, axis=1).astype(jnp.int32)
    moving = offset < SLOTS - 1
    stride = 1 + offset % (count - 1)
    own_inst = jnp.broadcast_to(jnp.arange(count, dtype=jnp.int32)[:, None], (count, SLOTS))
    own_slot = jnp.broadcast_to(jnp.arange(SLOTS, dtype=jnp.int32)[None, :], (count, SLOTS))
    target_inst = jnp.where(moving, order[(place[:, None] + stride) % count], own_inst).astype(jnp.int32)
    target_slot = jnp.where(moving, slot_perm[target_inst, offset], own_slot).astype(jnp.int32)
    return (target_inst.reshape(-1).astype(jnp.int32), target_slot.reshape(-1).astype(jnp.int32))


def draw_dest_inst(key, part):
    return plan_tables(key)[0]


def draw_dest_slot(key, part):
    return plan_tables(key)[1]


def draw_context_len(key, part):
    key = jax.random.fold_in(key, 5)
    lengths = jax.random.randint(key, (ROWS,), 1, CACHE - STEPS + 1)
    lengths = lengths.at[0].set(CACHE - STEPS).at[1].set(1)
    return lengths.astype(jnp.int32)


def draw_k_in(key, part):
    key = jax.random.fold_in(key, 11)
    noise = jnp.clip(jax.random.normal(key, (STEPS, ROWS, KVHEADS, HEAD_DIM), jnp.float32), -4.0, 4.0)
    return noise.reshape(STEPS, ROWS, KVHEADS * HEAD_DIM).astype(jnp.bfloat16)


def draw_q_in(key, part):
    key = jax.random.fold_in(key, 13)
    queries = jnp.clip(jax.random.normal(key, (STEPS, ROWS, QHEADS, HEAD_DIM), jnp.float32), -4.0, 4.0)
    return queries.reshape(STEPS, ROWS, QHEADS * HEAD_DIM).astype(jnp.bfloat16)


def block_scale(stream_key, shape, cuts, least, high):
    gain = 1.0
    for axis_at, shards_of in cuts:
        heights = jax.random.uniform(jax.random.fold_in(jax.random.fold_in(stream_key, 6), axis_at), (shards_of,), jnp.float32, least / len(cuts), high / len(cuts))
        gain = gain * jnp.repeat(jnp.exp(heights), shape[axis_at] // shards_of).reshape((-1,) + (1,) * (len(shape) - 1 - axis_at))
    return gain


def centred(key, shape, deviation, most, cuts=(), held_as=jnp.bfloat16):
    gain = block_scale(key, shape, cuts, -0.22, 0.18) if cuts else 1.0
    values = jax.random.normal(key, shape, jnp.float32) * deviation * gain
    return jnp.minimum(jnp.maximum(values, -most), most).astype(held_as)


def setup_inputs(seed: int = 0) -> dict:
    streams_of = jax.random.split(jax.random.key(seed), 23)
    ssm_state = centred(streams_of[0], (ROWS, MHEADS, HEAD_P, STATE_N), 1.0, 6.0, ((0, 8), (1, 4)))
    conv_x = centred(streams_of[1], (ROWS, CONV - 1, MHEADS * HEAD_P), 1.0, 6.0, ((0, 8), (2, 4)))
    conv_bc = centred(streams_of[2], (ROWS, CONV - 1, 2 * GROUPS * STATE_N), 1.0, 6.0, ((0, 8), (2, 4)))
    k_cache = centred(streams_of[3], (ROWS, CACHE, KVHEADS * HEAD_DIM), 1.0, 5.0, ((0, 8), (2, 4)))
    v_cache = centred(streams_of[4], (ROWS, CACHE, KVHEADS * HEAD_DIM), 1.0, 5.0, ((0, 8), (2, 4)))
    context_len = draw_context_len(jax.random.fold_in(streams_of[22], 71), 0)
    dest_inst = draw_dest_inst(jax.random.fold_in(streams_of[22], 71), 0)
    dest_slot = draw_dest_slot(jax.random.fold_in(streams_of[22], 71), 0)
    x_in = centred(streams_of[8], (STEPS, ROWS, MHEADS * HEAD_P), 1.0, 6.0, ((1, 8), (2, 4)))
    bc_in = centred(streams_of[9], (STEPS, ROWS, 2 * GROUPS * STATE_N), 1.0, 6.0, ((1, 8), (2, 4)))
    z_in = centred(streams_of[10], (STEPS, ROWS, MHEADS * HEAD_P), 1.0, 6.0, ((1, 8), (2, 4)))
    dt_in = centred(streams_of[11], (STEPS, ROWS, MHEADS), 1.0, 4.0, ((1, 8), (2, 4)), jnp.float32)
    q_in = draw_q_in(jax.random.fold_in(streams_of[22], 71), 0)
    k_in = draw_k_in(jax.random.fold_in(streams_of[22], 71), 0)
    v_in = centred(streams_of[14], (STEPS, ROWS, KVHEADS * HEAD_DIM), 1.0, 5.0, ((1, 8), (2, 4)))
    conv_wx = centred(streams_of[15], (CONV, MHEADS * HEAD_P), CONV ** -0.5, 3.0, ((1, 4),), jnp.float32)
    conv_wbc = centred(streams_of[16], (CONV, 2 * GROUPS * STATE_N), CONV ** -0.5, 3.0, ((1, 4),), jnp.float32)
    a_rate = jnp.clip(jnp.exp(math.log(3.0) - 5.0106353 * jax.random.uniform(streams_of[17], (MHEADS,), jnp.float32) ** block_scale(streams_of[17], (MHEADS,), ((0, 4),), -0.2, 0.2)), 0.02, 3.0)
    dt_bias = jnp.clip(jax.random.uniform(streams_of[18], (MHEADS,), jnp.float32, -1.0, 1.0) * block_scale(streams_of[18], (MHEADS,), ((0, 4),), -0.4, 0.0), -1.0, 1.0)
    d_skip = jnp.clip(1.0 + 3.0 * jax.random.uniform(streams_of[19], (MHEADS,), jnp.float32) ** block_scale(streams_of[19], (MHEADS,), ((0, 4),), -0.2, 0.2), 1.0, 4.0)
    norm_gain = jnp.clip(1.0 + 0.1 * jax.random.normal(streams_of[20], (MHEADS * HEAD_P,), jnp.float32), 0.5, 1.5).astype(jnp.bfloat16)
    o_proj = centred(streams_of[21], (QHEADS * HEAD_DIM, D), (QHEADS * HEAD_DIM) ** -0.5, 0.09375, ((0, 4),))
    return dict(ssm_state=ssm_state, conv_x=conv_x, conv_bc=conv_bc, k_cache=k_cache, v_cache=v_cache, context_len=context_len, dest_inst=dest_inst, dest_slot=dest_slot, x_in=x_in, bc_in=bc_in, z_in=z_in, dt_in=dt_in, q_in=q_in, k_in=k_in, v_in=v_in, conv_wx=conv_wx, conv_wbc=conv_wbc, a_rate=a_rate, dt_bias=dt_bias, d_skip=d_skip, norm_gain=norm_gain, o_proj=o_proj)


def reference(ssm_state, conv_x, conv_bc, k_cache, v_cache, context_len, dest_inst, dest_slot, x_in, bc_in, z_in, dt_in, q_in, k_in, v_in, conv_wx, conv_wbc, a_rate, dt_bias, d_skip, norm_gain, o_proj):
    target = (dest_inst * SLOTS + dest_slot).astype(jnp.int32)

    def migrate(source):
        return jnp.zeros_like(source).at[target].set(source)
    state_now = migrate(ssm_state)
    window_x = migrate(conv_x)
    window_bc = migrate(conv_bc)
    key_rows = migrate(k_cache)
    value_rows = migrate(v_cache)
    live_len = migrate(context_len)
    row_count = ROWS
    per_group = MHEADS // GROUPS
    query_group = QHEADS // KVHEADS
    score_scale = 1.0 / HEAD_DIM ** 0.5
    positions = jnp.arange(CACHE, dtype=jnp.int32)
    mamba_list = []
    attn_list = []
    for decode_step in range(STEPS):
        full_x = jnp.concatenate([window_x, x_in[decode_step][:, None, :]], axis=1)
        conv_out_x = jax.nn.silu(lax.optimization_barrier(jnp.sum(full_x.astype(jnp.float32) * conv_wx[None], axis=1)))
        window_x = full_x[:, 1:]
        full_bc = jnp.concatenate([window_bc, bc_in[decode_step][:, None, :]], axis=1)
        conv_out_bc = jax.nn.silu(lax.optimization_barrier(jnp.sum(full_bc.astype(jnp.float32) * conv_wbc[None], axis=1)))
        window_bc = full_bc[:, 1:]
        xs_heads = conv_out_x.reshape(row_count, MHEADS, HEAD_P)
        pairs = conv_out_bc.reshape(row_count, GROUPS, 2, STATE_N)
        b_heads = jnp.repeat(pairs[:, :, 0], per_group, axis=1)
        c_heads = jnp.repeat(pairs[:, :, 1], per_group, axis=1)
        delta = jax.nn.softplus(dt_in[decode_step] + dt_bias[None])
        decay = jnp.exp(-delta * a_rate[None])
        fresh = state_now.astype(jnp.float32) * decay[:, :, None, None] + (delta[:, :, None] * xs_heads)[:, :, :, None] * b_heads[:, :, None, :]
        y_heads = lax.optimization_barrier(jnp.sum(fresh * c_heads[:, :, None, :], axis=3)) + d_skip[None, :, None] * xs_heads
        state_now = fresh.astype(jnp.bfloat16)
        gated = y_heads.reshape(row_count, -1) * jax.nn.silu(z_in[decode_step].astype(jnp.float32))
        grouped = gated.reshape(row_count, GROUPS, -1)
        normed = grouped * lax.rsqrt(lax.optimization_barrier(jnp.mean(grouped * grouped, axis=2, keepdims=True)) + 1e-05)
        mamba_list.append((normed.reshape(row_count, -1) * norm_gain.astype(jnp.float32)[None]).astype(jnp.bfloat16))
        write_pos = live_len + decode_step
        written = positions[None, :, None] == write_pos[:, None, None]
        key_rows = jnp.where(written, k_in[decode_step][:, None, :], key_rows)
        value_rows = jnp.where(written, v_in[decode_step][:, None, :], value_rows)
        queries = q_in[decode_step].astype(jnp.float32).reshape(row_count, KVHEADS, query_group, HEAD_DIM)
        key_heads = key_rows.astype(jnp.float32).reshape(row_count, CACHE, KVHEADS, HEAD_DIM)
        value_heads = value_rows.astype(jnp.float32).reshape(row_count, CACHE, KVHEADS, HEAD_DIM)
        scores = jnp.einsum('rkgd,rckd->rkgc', queries, key_heads) * score_scale
        visible = positions[None, None, None, :] <= write_pos[:, None, None, None]
        scores = jnp.where(visible, scores, -jnp.inf)
        top_score = lax.optimization_barrier(jnp.max(scores, axis=3, keepdims=True))
        raised = jnp.exp(scores - top_score)
        weights = (raised / lax.optimization_barrier(jnp.sum(raised, axis=3, keepdims=True))).astype(jnp.bfloat16)
        mixed = jnp.einsum('rkgc,rckd->rkgd', weights.astype(jnp.float32), value_heads).astype(jnp.bfloat16)
        mixed = mixed.reshape(row_count, -1)
        attn_list.append(jnp.dot(mixed, o_proj, preferred_element_type=jnp.float32).astype(jnp.bfloat16))
    return (state_now, window_x, window_bc, key_rows, value_rows, jnp.stack(mamba_list), jnp.stack(attn_list))
```

```python
import functools

import jax
import jax.numpy as jnp
from jax import lax
from jax.experimental import pallas as pl
from jax.experimental.pallas import tpu as pltpu
from jax.sharding import PartitionSpec as P

STEPS = 3
QHEADS = 32
KVHEADS = 8
HEAD_DIM = 128
CHUNKS = (24, 8)


def pack_small_kernel(src_ref, row_ref, k_ref, v_ref, extra_ref, out_ref):
    cache_len = k_ref.shape[1]
    for b in range(out_ref.shape[0]):
        out_ref[b, :cache_len] = k_ref[src_ref[b]]
        out_ref[b, cache_len : 2 * cache_len] = v_ref[src_ref[b]]
        out_ref[b, 2 * cache_len :] = extra_ref[row_ref[b]]


def pack_state_kernel(buckets, src_ref, state_ref, *rest):
    outs, sems = rest[: len(CHUNKS)], rest[len(CHUNKS)]
    copies = []
    at = 0
    for c, heads in enumerate(CHUNKS):
        for b in range(buckets):
            copies.append(
                pltpu.make_async_copy(
                    state_ref.at[src_ref[b], pl.ds(at, heads)], outs[c].at[b], sems.at[c, b]
                )
            )
        at += heads
    for copy in copies:
        copy.start()
    for copy in copies:
        copy.wait()


def unpack_kernel(take_ref, got_ref, k_ref, v_ref, extra_ref):
    cache_len = k_ref.shape[1]
    for s in range(k_ref.shape[0]):
        k_ref[s] = got_ref[take_ref[s], :cache_len]
        v_ref[s] = got_ref[take_ref[s], cache_len : 2 * cache_len]
        extra_ref[s] = got_ref[take_ref[s], 2 * cache_len :]


def state_kernel(first, head_count, take_ref, carry_ref, got_ref, u_ref, b_ref, c_ref, *rest):
    final_ref, y_ref = rest[-2:]
    slot = pl.program_id(0)
    heads, size, width = got_ref.shape[1:]
    old = got_ref[0].reshape(heads * size, width)
    both = lax.dot_general(
        c_ref[0], old, (((1,), (1,)), ((), ())), preferred_element_type=jnp.float32
    )
    y_ref[0] = both[:8] + both[8:]
    added = lax.dot_general(
        u_ref[0], b_ref[0], (((0,), (0,)), ((), ())), preferred_element_type=jnp.float32
    )
    for h in range(heads):
        kept = got_ref[0, h].astype(jnp.float32) * carry_ref[slot * head_count + first + h]
        final_ref[0, h] = (kept + added[h * size : (h + 1) * size]).astype(jnp.bfloat16)


def split_two(value):
    high = lax.reduce_precision(value, 8, 7)
    return high.astype(jnp.bfloat16), (value - high).astype(jnp.bfloat16)


def on_device(
    ssm_state,
    conv_x,
    conv_bc,
    k_cache,
    v_cache,
    context_len,
    dest_inst,
    dest_slot,
    x_in,
    bc_in,
    z_in,
    dt_in,
    q_in,
    k_in,
    v_in,
    conv_wx,
    conv_wbc,
    a_rate,
    dt_bias,
    d_skip,
    norm_gain,
    o_proj,
):
    bf16, f32 = jnp.bfloat16, jnp.float32
    peer_count = lax.axis_size("inst")
    slot_count = context_len.shape[0]
    per_peer = (slot_count - 2) // (peer_count - 1) + 1
    buckets = peer_count * per_peer
    head_count, head_size, state_size = ssm_state.shape[1:]
    cache_len, kv_width = k_cache.shape[1:]
    channels = head_count * head_size
    anywhere = pl.BlockSpec(memory_space=pl.ANY)
    in_vmem = pl.BlockSpec(memory_space=pltpu.VMEM)
    in_smem = pl.BlockSpec(memory_space=pltpu.SMEM)

    slot_ids = jnp.arange(slot_count, dtype=jnp.int32)
    earlier = (dest_inst[None, :] == dest_inst[:, None]) & (slot_ids[None, :] < slot_ids[:, None])
    rank_here = jnp.sum(earlier.astype(jnp.int32), axis=1)
    bucket = dest_inst * per_peer + rank_here
    bucket_ids = jnp.arange(buckets, dtype=jnp.int32)
    chosen = bucket[None, :] == bucket_ids[:, None]
    row = jnp.min(jnp.where(chosen, slot_ids[None, :], slot_count), axis=1)
    src = jnp.where(row == slot_count, 0, row)

    x_rows = 3 * channels // kv_width
    bc_rows = 3 * conv_bc.shape[2] // kv_width
    used = x_rows + bc_rows
    extra_rows = -(-(used + 1) // 16) * 16
    plan = jnp.stack([dest_slot, context_len], axis=1).astype(bf16)
    plan = jnp.pad(plan, ((0, 1), (0, 0)), constant_values=-1)
    plan = jnp.pad(plan, ((0, 0), (0, kv_width - 2)))[:, None, :]
    extra = jnp.concatenate(
        [
            conv_x.reshape(slot_count, x_rows, kv_width),
            conv_bc.reshape(slot_count, bc_rows, kv_width),
        ],
        axis=1,
    )
    extra = jnp.concatenate([jnp.pad(extra, ((0, 1), (0, 0), (0, 0))), plan], axis=1)
    extra = jnp.pad(extra, ((0, 0), (0, extra_rows - used - 1), (0, 0)))
    small_rows = 2 * cache_len + extra_rows
    small = pl.pallas_call(
        pack_small_kernel,
        out_shape=jax.ShapeDtypeStruct((buckets, small_rows, kv_width), bf16),
        in_specs=[in_smem, in_smem, in_vmem, in_vmem, in_vmem],
        out_specs=in_vmem,
        cost_estimate=pl.CostEstimate(flops=0, bytes_accessed=4000000, transcendentals=0),
        compiler_params=pltpu.CompilerParams(vmem_limit_bytes=32 * 1024 * 1024),
    )(src, row, k_cache, v_cache, extra)
    packed = pl.pallas_call(
        functools.partial(pack_state_kernel, buckets),
        out_shape=[
            jax.ShapeDtypeStruct((buckets, heads, head_size, state_size), bf16) for heads in CHUNKS
        ],
        in_specs=[in_smem, anywhere],
        out_specs=[anywhere] * len(CHUNKS),
        scratch_shapes=[pltpu.SemaphoreType.DMA((len(CHUNKS), buckets))],
        cost_estimate=pl.CostEstimate(
            flops=0, bytes_accessed=4 * ssm_state.size, transcendentals=0
        ),
    )(src, ssm_state)

    got_small = lax.all_to_all(small, "inst", split_axis=0, concat_axis=0, tiled=True)
    got_state = [
        lax.all_to_all(part, "inst", split_axis=0, concat_axis=0, tiled=True) for part in packed
    ]

    arrived = got_small[:, 2 * cache_len + used, :2].astype(jnp.int32)
    hit = arrived[None, :, 0] == slot_ids[:, None]
    take = jnp.max(jnp.where(hit, bucket_ids[None, :], 0), axis=1)
    live_len = jnp.sum(jnp.where(hit, arrived[None, :, 1], 0), axis=1)
    key_rows, value_rows, extra_now = pl.pallas_call(
        unpack_kernel,
        out_shape=[
            jax.ShapeDtypeStruct(k_cache.shape, bf16),
            jax.ShapeDtypeStruct(v_cache.shape, bf16),
            jax.ShapeDtypeStruct((slot_count, extra_rows, kv_width), bf16),
        ],
        in_specs=[in_smem, in_vmem],
        out_specs=[in_vmem] * 3,
        cost_estimate=pl.CostEstimate(flops=0, bytes_accessed=4000000, transcendentals=0),
        compiler_params=pltpu.CompilerParams(vmem_limit_bytes=32 * 1024 * 1024),
    )(take, got_small)

    taps = conv_wx.shape[0]
    series_x = jnp.concatenate(
        [
            extra_now[:, :x_rows].reshape(slot_count, taps - 1, channels).transpose(1, 0, 2),
            x_in,
        ],
        axis=0,
    )
    series_bc = jnp.concatenate(
        [
            extra_now[:, x_rows:used].reshape(slot_count, taps - 1, -1).transpose(1, 0, 2),
            bc_in,
        ],
        axis=0,
    )
    window_x = series_x[STEPS:].transpose(1, 0, 2)
    window_bc = series_bc[STEPS:].transpose(1, 0, 2)

    def convolve(series, weights):
        total = sum(
            series[k : k + STEPS].astype(f32) * weights[k][None, None] for k in range(taps)
        )
        return jax.nn.silu(total)

    xs = convolve(series_x, conv_wx)
    conv_out_bc = convolve(series_bc, conv_wbc)
    b_vec, c_vec = conv_out_bc[..., :state_size], conv_out_bc[..., state_size:]
    delta = jax.nn.softplus(dt_in + dt_bias[None, None])
    decay = jnp.exp(-delta * a_rate[None, None])

    def spread(value):
        return jnp.repeat(value, head_size, axis=-1)

    reach = {}
    for first in range(STEPS):
        for last in range(first, STEPS):
            reach[first, last] = (
                decay[first] if first == last else reach[first, last - 1] * decay[last]
            )
    dots = {
        (i, t): jnp.sum(b_vec[i] * c_vec[t], axis=-1, keepdims=True)
        for t in range(STEPS)
        for i in range(t + 1)
    }
    y_new = []
    for t in range(STEPS):
        total = d_skip[None] + delta[t] * dots[t, t]
        part = xs[t] * spread(total)
        for i in range(t):
            part = part + xs[i] * spread(delta[i] * reach[i + 1, t] * dots[i, t])
        y_new.append(part)
    y_new = jnp.stack(y_new)
    grown = []
    for i in range(STEPS):
        scale = delta[i] if i == STEPS - 1 else delta[i] * reach[i + 1, STEPS - 1]
        grown.append(xs[i] * spread(scale))
    u_high, u_low = split_two(jnp.stack(grown, axis=1))
    b_high, b_low = split_two(b_vec.transpose(1, 0, 2))
    c_high, c_low = split_two(c_vec.transpose(1, 0, 2))
    u_all = jnp.pad(
        jnp.concatenate([u_high, u_high, u_low], axis=1), ((0, 0), (0, 16 - 3 * STEPS), (0, 0))
    )
    b_all = jnp.pad(
        jnp.concatenate([b_high, b_low, b_high], axis=1), ((0, 0), (0, 16 - 3 * STEPS), (0, 0))
    )
    eight = ((0, 0), (0, 8 - STEPS), (0, 0))
    c_all = jnp.concatenate([jnp.pad(c_high, eight), jnp.pad(c_low, eight)], axis=1)
    carry = reach[0, STEPS - 1].reshape(-1)
    gate = jax.nn.silu(z_in.astype(f32))
    y_scale = spread(jnp.stack([reach[0, t] for t in range(STEPS)]))
    gain = norm_gain.astype(f32)[None, None]

    kv_count = kv_width // HEAD_DIM
    query_group = QHEADS // KVHEADS
    positions = jnp.arange(cache_len, dtype=jnp.int32)
    for t in range(STEPS):
        written = positions[None, :, None] == (live_len + t)[:, None, None]
        key_rows = jnp.where(written, k_in[t][:, None, :], key_rows)
        value_rows = jnp.where(written, v_in[t][:, None, :], value_rows)
    queries = q_in.reshape(STEPS, slot_count, kv_count, query_group, HEAD_DIM)
    queries = queries.transpose(1, 2, 0, 3, 4).reshape(slot_count, kv_count, -1, HEAD_DIM)
    key_heads = key_rows.reshape(slot_count, cache_len, kv_count, HEAD_DIM)
    value_heads = value_rows.reshape(slot_count, cache_len, kv_count, HEAD_DIM)
    scores = jnp.einsum("skgd,sckd->skgc", queries, key_heads, preferred_element_type=f32)
    scores = scores * (1.0 / HEAD_DIM**0.5)
    row_step = jnp.arange(STEPS * query_group, dtype=jnp.int32) // query_group
    limit = live_len[:, None] + row_step[None, :]
    visible = positions[None, None, None, :] <= limit[:, None, :, None]
    scores = jnp.where(visible, scores, -jnp.inf)
    raised = jnp.exp(scores - jnp.max(scores, axis=3, keepdims=True))
    weights = (raised / jnp.sum(raised, axis=3, keepdims=True)).astype(bf16)
    mixed = jnp.einsum("skgc,sckd->skgd", weights, value_heads, preferred_element_type=f32)
    mixed = mixed.astype(bf16).reshape(slot_count, kv_count, STEPS, query_group, HEAD_DIM)
    mixed = mixed.transpose(2, 0, 1, 3, 4).reshape(STEPS * slot_count, -1)
    partial_value = jnp.dot(mixed, o_proj, preferred_element_type=f32)
    attn_all = lax.psum_scatter(
        partial_value.astype(bf16), "tp", scatter_dimension=1, tiled=True
    ).reshape(STEPS, slot_count, -1)

    final = None
    y_parts = []
    first = 0
    for heads, got in zip(CHUNKS, got_state):
        block = (1, heads, head_size, state_size)
        at = first // heads
        in_specs = [
            pl.BlockSpec(block, lambda s, take, carry: (take[s], 0, 0, 0)),
            pl.BlockSpec((1, 16, heads * head_size), lambda s, take, carry, at=at: (s, 0, at)),
            pl.BlockSpec((1, 16, state_size), lambda s, take, carry: (s, 0, 0)),
            pl.BlockSpec((1, 16, state_size), lambda s, take, carry: (s, 0, 0)),
        ]
        args = [take, carry, got, u_all, b_all, c_all]
        aliases = {}
        if final is not None:
            in_specs.append(anywhere)
            aliases = {len(args): 0}
            args.append(final)
        final, y_part = pl.pallas_call(
            functools.partial(state_kernel, first, head_count),
            grid_spec=pltpu.PrefetchScalarGridSpec(
                num_scalar_prefetch=2,
                grid=(slot_count,),
                in_specs=in_specs,
                out_specs=[
                    pl.BlockSpec(block, lambda s, take, carry, at=at: (s, at, 0, 0)),
                    pl.BlockSpec((1, 8, heads * head_size), lambda s, take, carry: (s, 0, 0)),
                ],
            ),
            out_shape=[
                jax.ShapeDtypeStruct(ssm_state.shape, bf16),
                jax.ShapeDtypeStruct((slot_count, 8, heads * head_size), f32),
            ],
            input_output_aliases=aliases,
            cost_estimate=pl.CostEstimate(
                flops=2 * 32 * got.size, bytes_accessed=4 * got.size, transcendentals=0
            ),
            compiler_params=pltpu.CompilerParams(vmem_limit_bytes=32 * 1024 * 1024),
        )(*args)
        y_parts.append(y_part[:, :STEPS].transpose(1, 0, 2))
        first += heads

    y_all = jnp.concatenate(y_parts, axis=2) * y_scale + y_new
    gated = y_all * gate
    normed = gated * lax.rsqrt(jnp.mean(gated * gated, axis=2, keepdims=True) + 1e-05)
    mamba = (normed * gain).astype(bf16)
    return (final, window_x, window_bc, key_rows, value_rows, mamba, attn_all)


def solution(mesh):
    in_specs = (
        P("inst", "tp", None, None),
        P("inst", None, "tp"),
        P("inst", None, "tp"),
        P("inst", None, "tp"),
        P("inst", None, "tp"),
        P("inst"),
        P("inst"),
        P("inst"),
        P(None, "inst", "tp"),
        P(None, "inst", "tp"),
        P(None, "inst", "tp"),
        P(None, "inst", "tp"),
        P(None, "inst", "tp"),
        P(None, "inst", "tp"),
        P(None, "inst", "tp"),
        P(None, "tp"),
        P(None, "tp"),
        P("tp"),
        P("tp"),
        P("tp"),
        P("tp"),
        P("tp", None),
    )
    out_specs = (
        P("inst", "tp", None, None),
        P("inst", None, "tp"),
        P("inst", None, "tp"),
        P("inst", None, "tp"),
        P("inst", None, "tp"),
        P(None, "inst", "tp"),
        P(None, "inst", "tp"),
    )
    return jax.shard_map(
        on_device, mesh=mesh, in_specs=in_specs, out_specs=out_specs, check_vma=False
    )
```

```python
import functools

import jax
import jax.numpy as jnp
from jax import lax
from jax.experimental import pallas as pl
from jax.experimental.pallas import tpu as pltpu
from jax.sharding import PartitionSpec as P

STEPS = 3
QHEADS = 32
KVHEADS = 8
HEAD_DIM = 128
CHUNKS = (24, 8)


def pack_small_kernel(src_ref, row_ref, k_ref, v_ref, extra_ref, out_ref):
    cache_len = k_ref.shape[1]
    for b in range(out_ref.shape[0]):
        out_ref[b, :cache_len] = k_ref[src_ref[b]]
        out_ref[b, cache_len : 2 * cache_len] = v_ref[src_ref[b]]
        out_ref[b, 2 * cache_len :] = extra_ref[row_ref[b]]


def pack_state_kernel(src_ref, state_ref, *outs):
    at = 0
    for heads, out in zip(CHUNKS, outs):
        out[0] = state_ref[0, at : at + heads]
        at += heads


def unpack_kernel(take_ref, got_ref, k_ref, v_ref, extra_ref):
    cache_len = k_ref.shape[1]
    for s in range(k_ref.shape[0]):
        k_ref[s] = got_ref[take_ref[s], :cache_len]
        v_ref[s] = got_ref[take_ref[s], cache_len : 2 * cache_len]
        extra_ref[s] = got_ref[take_ref[s], 2 * cache_len :]


def state_kernel(first, head_count, take_ref, carry_ref, got_ref, u_ref, b_ref, c_ref, *rest):
    final_ref, y_ref = rest[-2:]
    slot = pl.program_id(0)
    heads, size, width = got_ref.shape[1:]
    old = got_ref[0].reshape(heads * size, width)
    both = lax.dot_general(
        c_ref[0], old, (((1,), (1,)), ((), ())), preferred_element_type=jnp.float32
    )
    y_ref[0] = both[:8] + both[8:]
    added = lax.dot_general(
        u_ref[0], b_ref[0], (((0,), (0,)), ((), ())), preferred_element_type=jnp.float32
    )
    for h in range(heads):
        kept = got_ref[0, h].astype(jnp.float32) * carry_ref[slot * head_count + first + h]
        final_ref[0, h] = (kept + added[h * size : (h + 1) * size]).astype(jnp.bfloat16)


def split_two(value):
    high = lax.reduce_precision(value, 8, 7)
    return high.astype(jnp.bfloat16), (value - high).astype(jnp.bfloat16)


def on_device(
    ssm_state,
    conv_x,
    conv_bc,
    k_cache,
    v_cache,
    context_len,
    dest_inst,
    dest_slot,
    x_in,
    bc_in,
    z_in,
    dt_in,
    q_in,
    k_in,
    v_in,
    conv_wx,
    conv_wbc,
    a_rate,
    dt_bias,
    d_skip,
    norm_gain,
    o_proj,
):
    bf16, f32 = jnp.bfloat16, jnp.float32
    peer_count = lax.axis_size("inst")
    slot_count = context_len.shape[0]
    per_peer = (slot_count - 2) // (peer_count - 1) + 1
    buckets = peer_count * per_peer
    head_count, head_size, state_size = ssm_state.shape[1:]
    cache_len, kv_width = k_cache.shape[1:]
    channels = head_count * head_size
    anywhere = pl.BlockSpec(memory_space=pl.ANY)
    in_vmem = pl.BlockSpec(memory_space=pltpu.VMEM)
    in_smem = pl.BlockSpec(memory_space=pltpu.SMEM)

    slot_ids = jnp.arange(slot_count, dtype=jnp.int32)
    earlier = (dest_inst[None, :] == dest_inst[:, None]) & (slot_ids[None, :] < slot_ids[:, None])
    rank_here = jnp.sum(earlier.astype(jnp.int32), axis=1)
    bucket = dest_inst * per_peer + rank_here
    bucket_ids = jnp.arange(buckets, dtype=jnp.int32)
    chosen = bucket[None, :] == bucket_ids[:, None]
    row = jnp.min(jnp.where(chosen, slot_ids[None, :], slot_count), axis=1)
    src = jnp.where(row == slot_count, 0, row)

    x_rows = 3 * channels // kv_width
    bc_rows = 3 * conv_bc.shape[2] // kv_width
    used = x_rows + bc_rows
    extra_rows = -(-(used + 1) // 16) * 16
    plan = jnp.stack([dest_slot, context_len], axis=1).astype(bf16)
    plan = jnp.pad(plan, ((0, 1), (0, 0)), constant_values=-1)
    plan = jnp.pad(plan, ((0, 0), (0, kv_width - 2)))[:, None, :]
    extra = jnp.concatenate(
        [
            conv_x.reshape(slot_count, x_rows, kv_width),
            conv_bc.reshape(slot_count, bc_rows, kv_width),
        ],
        axis=1,
    )
    extra = jnp.concatenate([jnp.pad(extra, ((0, 1), (0, 0), (0, 0))), plan], axis=1)
    extra = jnp.pad(extra, ((0, 0), (0, extra_rows - used - 1), (0, 0)))
    small_rows = 2 * cache_len + extra_rows
    small = pl.pallas_call(
        pack_small_kernel,
        out_shape=jax.ShapeDtypeStruct((buckets, small_rows, kv_width), bf16),
        in_specs=[in_smem, in_smem, in_vmem, in_vmem, in_vmem],
        out_specs=in_vmem,
        cost_estimate=pl.CostEstimate(flops=0, bytes_accessed=4000000, transcendentals=0),
        compiler_params=pltpu.CompilerParams(vmem_limit_bytes=32 * 1024 * 1024),
    )(src, row, k_cache, v_cache, extra)
    packed = pl.pallas_call(
        pack_state_kernel,
        grid_spec=pltpu.PrefetchScalarGridSpec(
            num_scalar_prefetch=1,
            grid=(buckets,),
            in_specs=[
                pl.BlockSpec(
                    (1, head_count, head_size, state_size), lambda b, src: (src[b], 0, 0, 0)
                )
            ],
            out_specs=[
                pl.BlockSpec((1, heads, head_size, state_size), lambda b, src: (b, 0, 0, 0))
                for heads in CHUNKS
            ],
        ),
        out_shape=[
            jax.ShapeDtypeStruct((buckets, heads, head_size, state_size), bf16) for heads in CHUNKS
        ],
        cost_estimate=pl.CostEstimate(
            flops=0, bytes_accessed=4 * ssm_state.size, transcendentals=0
        ),
        compiler_params=pltpu.CompilerParams(vmem_limit_bytes=32 * 1024 * 1024),
    )(src, ssm_state)

    got_small = lax.all_to_all(small, "inst", split_axis=0, concat_axis=0, tiled=True)
    got_state = [
        lax.all_to_all(part, "inst", split_axis=0, concat_axis=0, tiled=True) for part in packed
    ]

    arrived = got_small[:, 2 * cache_len + used, :2].astype(jnp.int32)
    hit = arrived[None, :, 0] == slot_ids[:, None]
    take = jnp.max(jnp.where(hit, bucket_ids[None, :], 0), axis=1)
    live_len = jnp.sum(jnp.where(hit, arrived[None, :, 1], 0), axis=1)
    key_rows, value_rows, extra_now = pl.pallas_call(
        unpack_kernel,
        out_shape=[
            jax.ShapeDtypeStruct(k_cache.shape, bf16),
            jax.ShapeDtypeStruct(v_cache.shape, bf16),
            jax.ShapeDtypeStruct((slot_count, extra_rows, kv_width), bf16),
        ],
        in_specs=[in_smem, in_vmem],
        out_specs=[in_vmem] * 3,
        cost_estimate=pl.CostEstimate(flops=0, bytes_accessed=4000000, transcendentals=0),
        compiler_params=pltpu.CompilerParams(vmem_limit_bytes=32 * 1024 * 1024),
    )(take, got_small)

    taps = conv_wx.shape[0]
    series_x = jnp.concatenate(
        [
            extra_now[:, :x_rows].reshape(slot_count, taps - 1, channels).transpose(1, 0, 2),
            x_in,
        ],
        axis=0,
    )
    series_bc = jnp.concatenate(
        [
            extra_now[:, x_rows:used].reshape(slot_count, taps - 1, -1).transpose(1, 0, 2),
            bc_in,
        ],
        axis=0,
    )
    window_x = series_x[STEPS:].transpose(1, 0, 2)
    window_bc = series_bc[STEPS:].transpose(1, 0, 2)

    def convolve(series, weights):
        total = sum(
            series[k : k + STEPS].astype(f32) * weights[k][None, None] for k in range(taps)
        )
        return jax.nn.silu(total)

    xs = convolve(series_x, conv_wx)
    conv_out_bc = convolve(series_bc, conv_wbc)
    b_vec, c_vec = conv_out_bc[..., :state_size], conv_out_bc[..., state_size:]
    delta = jax.nn.softplus(dt_in + dt_bias[None, None])
    decay = jnp.exp(-delta * a_rate[None, None])

    def spread(value):
        return jnp.repeat(value, head_size, axis=-1)

    reach = {}
    for first in range(STEPS):
        for last in range(first, STEPS):
            reach[first, last] = (
                decay[first] if first == last else reach[first, last - 1] * decay[last]
            )
    dots = {
        (i, t): jnp.sum(b_vec[i] * c_vec[t], axis=-1, keepdims=True)
        for t in range(STEPS)
        for i in range(t + 1)
    }
    y_new = []
    for t in range(STEPS):
        total = d_skip[None] + delta[t] * dots[t, t]
        part = xs[t] * spread(total)
        for i in range(t):
            part = part + xs[i] * spread(delta[i] * reach[i + 1, t] * dots[i, t])
        y_new.append(part)
    y_new = jnp.stack(y_new)
    grown = []
    for i in range(STEPS):
        scale = delta[i] if i == STEPS - 1 else delta[i] * reach[i + 1, STEPS - 1]
        grown.append(xs[i] * spread(scale))
    u_high, u_low = split_two(jnp.stack(grown, axis=1))
    b_high, b_low = split_two(b_vec.transpose(1, 0, 2))
    c_high, c_low = split_two(c_vec.transpose(1, 0, 2))
    u_all = jnp.pad(
        jnp.concatenate([u_high, u_high, u_low], axis=1), ((0, 0), (0, 16 - 3 * STEPS), (0, 0))
    )
    b_all = jnp.pad(
        jnp.concatenate([b_high, b_low, b_high], axis=1), ((0, 0), (0, 16 - 3 * STEPS), (0, 0))
    )
    eight = ((0, 0), (0, 8 - STEPS), (0, 0))
    c_all = jnp.concatenate([jnp.pad(c_high, eight), jnp.pad(c_low, eight)], axis=1)
    carry = reach[0, STEPS - 1].reshape(-1)
    gate = jax.nn.silu(z_in.astype(f32))
    y_scale = spread(jnp.stack([reach[0, t] for t in range(STEPS)]))
    gain = norm_gain.astype(f32)[None, None]

    kv_count = kv_width // HEAD_DIM
    query_group = QHEADS // KVHEADS
    positions = jnp.arange(cache_len, dtype=jnp.int32)
    for t in range(STEPS):
        written = positions[None, :, None] == (live_len + t)[:, None, None]
        key_rows = jnp.where(written, k_in[t][:, None, :], key_rows)
        value_rows = jnp.where(written, v_in[t][:, None, :], value_rows)
    queries = q_in.reshape(STEPS, slot_count, kv_count, query_group, HEAD_DIM)
    queries = queries.transpose(1, 2, 0, 3, 4).reshape(slot_count, kv_count, -1, HEAD_DIM)
    key_heads = key_rows.reshape(slot_count, cache_len, kv_count, HEAD_DIM)
    value_heads = value_rows.reshape(slot_count, cache_len, kv_count, HEAD_DIM)
    scores = jnp.einsum("skgd,sckd->skgc", queries, key_heads, preferred_element_type=f32)
    scores = scores * (1.0 / HEAD_DIM**0.5)
    row_step = jnp.arange(STEPS * query_group, dtype=jnp.int32) // query_group
    limit = live_len[:, None] + row_step[None, :]
    visible = positions[None, None, None, :] <= limit[:, None, :, None]
    scores = jnp.where(visible, scores, -jnp.inf)
    raised = jnp.exp(scores - jnp.max(scores, axis=3, keepdims=True))
    weights = (raised / jnp.sum(raised, axis=3, keepdims=True)).astype(bf16)
    mixed = jnp.einsum("skgc,sckd->skgd", weights, value_heads, preferred_element_type=f32)
    mixed = mixed.astype(bf16).reshape(slot_count, kv_count, STEPS, query_group, HEAD_DIM)
    mixed = mixed.transpose(2, 0, 1, 3, 4).reshape(STEPS * slot_count, -1)
    partial_value = jnp.dot(mixed, o_proj, preferred_element_type=f32)
    attn_all = lax.psum_scatter(
        partial_value.astype(bf16), "tp", scatter_dimension=1, tiled=True
    ).reshape(STEPS, slot_count, -1)

    final = None
    y_parts = []
    first = 0
    for heads, got in zip(CHUNKS, got_state):
        block = (1, heads, head_size, state_size)
        at = first // heads
        in_specs = [
            pl.BlockSpec(block, lambda s, take, carry: (take[s], 0, 0, 0)),
            pl.BlockSpec((1, 16, heads * head_size), lambda s, take, carry, at=at: (s, 0, at)),
            pl.BlockSpec((1, 16, state_size), lambda s, take, carry: (s, 0, 0)),
            pl.BlockSpec((1, 16, state_size), lambda s, take, carry: (s, 0, 0)),
        ]
        args = [take, carry, got, u_all, b_all, c_all]
        aliases = {}
        if final is not None:
            in_specs.append(anywhere)
            aliases = {len(args): 0}
            args.append(final)
        final, y_part = pl.pallas_call(
            functools.partial(state_kernel, first, head_count),
            grid_spec=pltpu.PrefetchScalarGridSpec(
                num_scalar_prefetch=2,
                grid=(slot_count,),
                in_specs=in_specs,
                out_specs=[
                    pl.BlockSpec(block, lambda s, take, carry, at=at: (s, at, 0, 0)),
                    pl.BlockSpec((1, 8, heads * head_size), lambda s, take, carry: (s, 0, 0)),
                ],
            ),
            out_shape=[
                jax.ShapeDtypeStruct(ssm_state.shape, bf16),
                jax.ShapeDtypeStruct((slot_count, 8, heads * head_size), f32),
            ],
            input_output_aliases=aliases,
            cost_estimate=pl.CostEstimate(
                flops=2 * 32 * got.size, bytes_accessed=4 * got.size, transcendentals=0
            ),
            compiler_params=pltpu.CompilerParams(vmem_limit_bytes=32 * 1024 * 1024),
        )(*args)
        y_parts.append(y_part[:, :STEPS].transpose(1, 0, 2))
        first += heads

    y_all = jnp.concatenate(y_parts, axis=2) * y_scale + y_new
    gated = y_all * gate
    normed = gated * lax.rsqrt(jnp.mean(gated * gated, axis=2, keepdims=True) + 1e-05)
    mamba = (normed * gain).astype(bf16)
    return (final, window_x, window_bc, key_rows, value_rows, mamba, attn_all)


def solution(mesh):
    in_specs = (
        P("inst", "tp", None, None),
        P("inst", None, "tp"),
        P("inst", None, "tp"),
        P("inst", None, "tp"),
        P("inst", None, "tp"),
        P("inst"),
        P("inst"),
        P("inst"),
        P(None, "inst", "tp"),
        P(None, "inst", "tp"),
        P(None, "inst", "tp"),
        P(None, "inst", "tp"),
        P(None, "inst", "tp"),
        P(None, "inst", "tp"),
        P(None, "inst", "tp"),
        P(None, "tp"),
        P(None, "tp"),
        P("tp"),
        P("tp"),
        P("tp"),
        P("tp"),
        P("tp", None),
    )
    out_specs = (
        P("inst", "tp", None, None),
        P("inst", None, "tp"),
        P("inst", None, "tp"),
        P("inst", None, "tp"),
        P("inst", None, "tp"),
        P(None, "inst", "tp"),
        P(None, "inst", "tp"),
    )
    return jax.shard_map(
        on_device, mesh=mesh, in_specs=in_specs, out_specs=out_specs, check_vma=False
    )
```

```python
import functools

import jax
import jax.numpy as jnp
from jax import lax
from jax.experimental import pallas as pl
from jax.experimental.pallas import tpu as pltpu
from jax.sharding import PartitionSpec as P

STEPS = 3
QHEADS = 32
KVHEADS = 8
HEAD_DIM = 128
CHUNKS = (28, 4)


def pack_small_kernel(src_ref, row_ref, k_ref, v_ref, extra_ref, out_ref):
    cache_len = k_ref.shape[1]
    for b in range(out_ref.shape[0]):
        out_ref[b, :cache_len] = k_ref[src_ref[b]]
        out_ref[b, cache_len : 2 * cache_len] = v_ref[src_ref[b]]
        out_ref[b, 2 * cache_len :] = extra_ref[row_ref[b]]


def pack_state_kernel(src_ref, state_ref, *outs):
    at = 0
    for heads, out in zip(CHUNKS, outs):
        out[0] = state_ref[0, at : at + heads]
        at += heads


def unpack_kernel(take_ref, got_ref, k_ref, v_ref, extra_ref):
    cache_len = k_ref.shape[1]
    for s in range(k_ref.shape[0]):
        k_ref[s] = got_ref[take_ref[s], :cache_len]
        v_ref[s] = got_ref[take_ref[s], cache_len : 2 * cache_len]
        extra_ref[s] = got_ref[take_ref[s], 2 * cache_len :]


def state_kernel(first, head_count, take_ref, carry_ref, got_ref, u_ref, b_ref, c_ref, *rest):
    final_ref, y_ref = rest[-2:]
    slots = final_ref.shape[0]
    heads, size, width = got_ref.shape[1:]
    for s in range(slots):
        slot = pl.program_id(0) * slots + s
        source = 0 if slots == 1 else take_ref[slot]
        old = got_ref[source]
        both = lax.dot_general(
            c_ref[s],
            old.reshape(heads * size, width),
            (((1,), (1,)), ((), ())),
            preferred_element_type=jnp.float32,
        )
        y_ref[s] = both[:8] + both[8:]
        added = lax.dot_general(
            u_ref[s], b_ref[s], (((0,), (0,)), ((), ())), preferred_element_type=jnp.float32
        )
        for h in range(heads):
            kept = old[h].astype(jnp.float32) * carry_ref[slot * head_count + first + h]
            new = kept + added[h * size : (h + 1) * size]
            final_ref[s, h] = new.astype(jnp.bfloat16)


def split_two(value):
    high = lax.reduce_precision(value, 8, 7)
    return high.astype(jnp.bfloat16), (value - high).astype(jnp.bfloat16)


def on_device(
    ssm_state,
    conv_x,
    conv_bc,
    k_cache,
    v_cache,
    context_len,
    dest_inst,
    dest_slot,
    x_in,
    bc_in,
    z_in,
    dt_in,
    q_in,
    k_in,
    v_in,
    conv_wx,
    conv_wbc,
    a_rate,
    dt_bias,
    d_skip,
    norm_gain,
    o_proj,
):
    bf16, f32 = jnp.bfloat16, jnp.float32
    peer_count = lax.axis_size("inst")
    slot_count = context_len.shape[0]
    per_peer = (slot_count - 2) // (peer_count - 1) + 1
    buckets = peer_count * per_peer
    head_count, head_size, state_size = ssm_state.shape[1:]
    cache_len, kv_width = k_cache.shape[1:]
    channels = head_count * head_size
    anywhere = pl.BlockSpec(memory_space=pl.ANY)
    in_vmem = pl.BlockSpec(memory_space=pltpu.VMEM)
    in_smem = pl.BlockSpec(memory_space=pltpu.SMEM)

    slot_ids = jnp.arange(slot_count, dtype=jnp.int32)
    earlier = (dest_inst[None, :] == dest_inst[:, None]) & (slot_ids[None, :] < slot_ids[:, None])
    rank_here = jnp.sum(earlier.astype(jnp.int32), axis=1)
    bucket = dest_inst * per_peer + rank_here
    bucket_ids = jnp.arange(buckets, dtype=jnp.int32)
    chosen = bucket[None, :] == bucket_ids[:, None]
    row = jnp.min(jnp.where(chosen, slot_ids[None, :], slot_count), axis=1)
    src = jnp.where(row == slot_count, 0, row)

    x_rows = 3 * channels // kv_width
    bc_rows = 3 * conv_bc.shape[2] // kv_width
    used = x_rows + bc_rows
    extra_rows = -(-(used + 1) // 16) * 16
    plan = jnp.stack([dest_slot, context_len], axis=1).astype(bf16)
    plan = jnp.pad(plan, ((0, 1), (0, 0)), constant_values=-1)
    plan = jnp.pad(plan, ((0, 0), (0, kv_width - 2)))[:, None, :]
    extra = jnp.concatenate(
        [
            conv_x.reshape(slot_count, x_rows, kv_width),
            conv_bc.reshape(slot_count, bc_rows, kv_width),
        ],
        axis=1,
    )
    extra = jnp.concatenate([jnp.pad(extra, ((0, 1), (0, 0), (0, 0))), plan], axis=1)
    extra = jnp.pad(extra, ((0, 0), (0, extra_rows - used - 1), (0, 0)))
    small_rows = 2 * cache_len + extra_rows
    small = pl.pallas_call(
        pack_small_kernel,
        out_shape=jax.ShapeDtypeStruct((buckets, small_rows, kv_width), bf16),
        in_specs=[in_smem, in_smem, in_vmem, in_vmem, in_vmem],
        out_specs=in_vmem,
        cost_estimate=pl.CostEstimate(flops=0, bytes_accessed=4000000, transcendentals=0),
        compiler_params=pltpu.CompilerParams(vmem_limit_bytes=32 * 1024 * 1024),
    )(src, row, k_cache, v_cache, extra)
    packed = pl.pallas_call(
        pack_state_kernel,
        grid_spec=pltpu.PrefetchScalarGridSpec(
            num_scalar_prefetch=1,
            grid=(buckets,),
            in_specs=[
                pl.BlockSpec(
                    (1, head_count, head_size, state_size), lambda b, src: (src[b], 0, 0, 0)
                )
            ],
            out_specs=[
                pl.BlockSpec((1, heads, head_size, state_size), lambda b, src: (b, 0, 0, 0))
                for heads in CHUNKS
            ],
        ),
        out_shape=[
            jax.ShapeDtypeStruct((buckets, heads, head_size, state_size), bf16) for heads in CHUNKS
        ],
        cost_estimate=pl.CostEstimate(
            flops=0, bytes_accessed=4 * ssm_state.size, transcendentals=0
        ),
        compiler_params=pltpu.CompilerParams(vmem_limit_bytes=32 * 1024 * 1024),
    )(src, ssm_state)

    got_small = lax.all_to_all(small, "inst", split_axis=0, concat_axis=0, tiled=True)

    arrived = got_small[:, 2 * cache_len + used, :2].astype(jnp.int32)
    hit = arrived[None, :, 0] == slot_ids[:, None]
    take = jnp.max(jnp.where(hit, bucket_ids[None, :], 0), axis=1)
    live_len = jnp.sum(jnp.where(hit, arrived[None, :, 1], 0), axis=1)
    key_rows, value_rows, extra_now = pl.pallas_call(
        unpack_kernel,
        out_shape=[
            jax.ShapeDtypeStruct(k_cache.shape, bf16),
            jax.ShapeDtypeStruct(v_cache.shape, bf16),
            jax.ShapeDtypeStruct((slot_count, extra_rows, kv_width), bf16),
        ],
        in_specs=[in_smem, in_vmem],
        out_specs=[in_vmem] * 3,
        cost_estimate=pl.CostEstimate(flops=0, bytes_accessed=4000000, transcendentals=0),
        compiler_params=pltpu.CompilerParams(vmem_limit_bytes=32 * 1024 * 1024),
    )(take, got_small)

    taps = conv_wx.shape[0]
    series_x = jnp.concatenate(
        [
            extra_now[:, :x_rows].reshape(slot_count, taps - 1, channels).transpose(1, 0, 2),
            x_in,
        ],
        axis=0,
    )
    series_bc = jnp.concatenate(
        [
            extra_now[:, x_rows:used].reshape(slot_count, taps - 1, -1).transpose(1, 0, 2),
            bc_in,
        ],
        axis=0,
    )
    window_x = series_x[STEPS:].transpose(1, 0, 2)
    window_bc = series_bc[STEPS:].transpose(1, 0, 2)

    def convolve(series, weights):
        total = sum(
            series[k : k + STEPS].astype(f32) * weights[k][None, None] for k in range(taps)
        )
        return jax.nn.silu(total)

    xs = convolve(series_x, conv_wx)
    conv_out_bc = convolve(series_bc, conv_wbc)
    b_vec, c_vec = conv_out_bc[..., :state_size], conv_out_bc[..., state_size:]
    delta = jax.nn.softplus(dt_in + dt_bias[None, None])
    decay = jnp.exp(-delta * a_rate[None, None])

    def spread(value):
        return jnp.repeat(value, head_size, axis=-1)

    reach = {}
    for first in range(STEPS):
        for last in range(first, STEPS):
            reach[first, last] = (
                decay[first] if first == last else reach[first, last - 1] * decay[last]
            )
    dots = {
        (i, t): jnp.sum(b_vec[i] * c_vec[t], axis=-1, keepdims=True)
        for t in range(STEPS)
        for i in range(t + 1)
    }
    y_new = []
    for t in range(STEPS):
        total = d_skip[None] + delta[t] * dots[t, t]
        part = xs[t] * spread(total)
        for i in range(t):
            part = part + xs[i] * spread(delta[i] * reach[i + 1, t] * dots[i, t])
        y_new.append(part)
    y_new = jnp.stack(y_new)
    grown = []
    for i in range(STEPS):
        scale = delta[i] if i == STEPS - 1 else delta[i] * reach[i + 1, STEPS - 1]
        grown.append(xs[i] * spread(scale))
    u_high, u_low = split_two(jnp.stack(grown, axis=1))
    b_high, b_low = split_two(b_vec.transpose(1, 0, 2))
    c_high, c_low = split_two(c_vec.transpose(1, 0, 2))
    u_all = jnp.pad(
        jnp.concatenate([u_high, u_high, u_low], axis=1), ((0, 0), (0, 16 - 3 * STEPS), (0, 0))
    )
    b_all = jnp.pad(
        jnp.concatenate([b_high, b_low, b_high], axis=1), ((0, 0), (0, 16 - 3 * STEPS), (0, 0))
    )
    eight = ((0, 0), (0, 8 - STEPS), (0, 0))
    c_all = jnp.concatenate([jnp.pad(c_high, eight), jnp.pad(c_low, eight)], axis=1)
    carry = reach[0, STEPS - 1].reshape(-1)
    gate = jax.nn.silu(z_in.astype(f32))
    y_scale = spread(jnp.stack([reach[0, t] for t in range(STEPS)]))
    gain = norm_gain.astype(f32)[None, None]

    kv_count = kv_width // HEAD_DIM
    query_group = QHEADS // KVHEADS
    positions = jnp.arange(cache_len, dtype=jnp.int32)
    for t in range(STEPS):
        written = positions[None, :, None] == (live_len + t)[:, None, None]
        key_rows = jnp.where(written, k_in[t][:, None, :], key_rows)
        value_rows = jnp.where(written, v_in[t][:, None, :], value_rows)
    queries = q_in.reshape(STEPS, slot_count, kv_count, query_group, HEAD_DIM)
    queries = queries.transpose(1, 2, 0, 3, 4).reshape(slot_count, kv_count, -1, HEAD_DIM)
    key_heads = key_rows.reshape(slot_count, cache_len, kv_count, HEAD_DIM)
    value_heads = value_rows.reshape(slot_count, cache_len, kv_count, HEAD_DIM)
    scores = jnp.einsum("skgd,sckd->skgc", queries, key_heads, preferred_element_type=f32)
    scores = scores * (1.0 / HEAD_DIM**0.5)
    row_step = jnp.arange(STEPS * query_group, dtype=jnp.int32) // query_group
    limit = live_len[:, None] + row_step[None, :]
    visible = positions[None, None, None, :] <= limit[:, None, :, None]
    scores = jnp.where(visible, scores, -jnp.inf)
    raised = jnp.exp(scores - jnp.max(scores, axis=3, keepdims=True))
    weights = (raised / jnp.sum(raised, axis=3, keepdims=True)).astype(bf16)
    mixed = jnp.einsum("skgc,sckd->skgd", weights, value_heads, preferred_element_type=f32)
    mixed = mixed.astype(bf16).reshape(slot_count, kv_count, STEPS, query_group, HEAD_DIM)
    mixed = mixed.transpose(2, 0, 1, 3, 4).reshape(STEPS * slot_count, -1)
    partial_value = jnp.dot(mixed, o_proj, preferred_element_type=f32)
    attn_all = lax.psum_scatter(
        partial_value.astype(bf16), "tp", scatter_dimension=1, tiled=True
    ).reshape(STEPS, slot_count, -1)

    tied = (packed[-1], attn_all, take, carry, u_all, b_all, c_all, y_new, y_scale, gate)
    tied = lax.optimization_barrier((*tied, window_x, window_bc, gain))
    last_part, attn_all, take, carry, u_all, b_all, c_all, y_new, y_scale, gate = tied[:10]
    window_x, window_bc, gain = tied[10:]
    got_state = [
        lax.all_to_all(part, "inst", split_axis=0, concat_axis=0, tiled=True)
        for part in [*packed[:-1], last_part]
    ]

    final = None
    y_parts = []
    first = 0
    for heads, got in zip(CHUNKS, got_state):
        at = first // heads
        slots = slot_count if final is not None else 1
        block = (slots, heads, head_size, state_size)
        if slots == 1:
            got_spec = pl.BlockSpec(block, lambda s, take, carry: (take[s], 0, 0, 0))
        else:
            got_spec = pl.BlockSpec(got.shape, lambda s, take, carry: (0, 0, 0, 0))
        in_specs = [
            got_spec,
            pl.BlockSpec((slots, 16, heads * head_size), lambda s, take, carry, at=at: (s, 0, at)),
            pl.BlockSpec((slots, 16, state_size), lambda s, take, carry: (s, 0, 0)),
            pl.BlockSpec((slots, 16, state_size), lambda s, take, carry: (s, 0, 0)),
        ]
        args = [take, carry, got, u_all, b_all, c_all]
        aliases = {}
        if final is not None:
            in_specs.append(anywhere)
            aliases = {len(args): 0}
            args.append(final)
        final, y_part = pl.pallas_call(
            functools.partial(state_kernel, first, head_count),
            grid_spec=pltpu.PrefetchScalarGridSpec(
                num_scalar_prefetch=2,
                grid=(slot_count // slots,),
                in_specs=in_specs,
                out_specs=[
                    pl.BlockSpec(block, lambda s, take, carry, at=at: (s, at, 0, 0)),
                    pl.BlockSpec((slots, 8, heads * head_size), lambda s, take, carry: (s, 0, 0)),
                ],
            ),
            out_shape=[
                jax.ShapeDtypeStruct(ssm_state.shape, bf16),
                jax.ShapeDtypeStruct((slot_count, 8, heads * head_size), f32),
            ],
            input_output_aliases=aliases,
            cost_estimate=pl.CostEstimate(
                flops=2 * 32 * got.size, bytes_accessed=4 * got.size, transcendentals=0
            ),
            compiler_params=pltpu.CompilerParams(vmem_limit_bytes=32 * 1024 * 1024),
        )(*args)
        y_parts.append(y_part[:, :STEPS].transpose(1, 0, 2))
        first += heads

    y_all = jnp.concatenate(y_parts, axis=2) * y_scale + y_new
    gated = y_all * gate
    normed = gated * lax.rsqrt(jnp.mean(gated * gated, axis=2, keepdims=True) + 1e-05)
    mamba = (normed * gain).astype(bf16)
    return (final, window_x, window_bc, key_rows, value_rows, mamba, attn_all)


def solution(mesh):
    in_specs = (
        P("inst", "tp", None, None),
        P("inst", None, "tp"),
        P("inst", None, "tp"),
        P("inst", None, "tp"),
        P("inst", None, "tp"),
        P("inst"),
        P("inst"),
        P("inst"),
        P(None, "inst", "tp"),
        P(None, "inst", "tp"),
        P(None, "inst", "tp"),
        P(None, "inst", "tp"),
        P(None, "inst", "tp"),
        P(None, "inst", "tp"),
        P(None, "inst", "tp"),
        P(None, "tp"),
        P(None, "tp"),
        P("tp"),
        P("tp"),
        P("tp"),
        P("tp"),
        P("tp", None),
    )
    out_specs = (
        P("inst", "tp", None, None),
        P("inst", None, "tp"),
        P("inst", None, "tp"),
        P("inst", None, "tp"),
        P("inst", None, "tp"),
        P(None, "inst", "tp"),
        P(None, "inst", "tp"),
    )
    return jax.shard_map(
        on_device, mesh=mesh, in_specs=in_specs, out_specs=out_specs, check_vma=False
    )
```
